128 devices in a mesh: row: 8 (over z, core), col: 16 (over x, y).
Axes of the slice: x: 4, y: 4, z: 4, core: 2. Of those that a mesh axis runs over, the one named last changes fastest.
Arguments:
- tokens: float32 [896, 8192], P('row', 'col'), may hold values from -6 to 6
- layer_norm_gain: float32 [8192], P('col'), may hold values from 0.1 to 1.9
- gate_alpha: float32 [1], replicated, may hold values from 0.3 to 1.2
- weight_in: float32 [8192, 16384], P('col', 'row'), may hold values from -0.0625 to 0.0625
- weight_out: float32 [16384, 8192], P('row', 'col'), may hold values from -0.046875 to 0.046875
- output_gradient: float32 [896, 8192], P('row', 'col'), may hold values from -6 to 6
Outputs:
- block_out: float32 [896, 8192], P('row', 'col')
- token_gradient: float32 [896, 8192], P('row', 'col')
- weight_in_grad: float32 [8192, 16384], P('col', 'row')
- weight_out_grad: float32 [16384, 8192], P('row', 'col')
- norm_gain_gradient: float32 [8192], P('col')
The draws below stay inside these ranges and needn't reach their ends.
All inputs are finite; a program needn't handle non-finite values.
Results may differ from the reference program's by a relative error of at most 0.000092.
Values sent between devices are 32-bit elements; how exact they have to be, the bound alone decides.
No kernel may reach another device: no remote copies, remote signals or barrier semaphores. Data moves between devices by JAX's collectives and lax.ppermute only.
A program may use at most 128 MiB of HBM per device.

```python
import jax
import jax.numpy as jnp
from jax import lax

D = 8192
FF = 16384
TOKENS = 896


def level_of(own_key, dims, shards, low, high):
    level = 1.0
    for position, blocks in shards:
        steps = jax.random.uniform(jax.random.fold_in(jax.random.fold_in(own_key, 6), position), (blocks,), jnp.float32, low / len(shards), high / len(shards))
        level = level * jnp.repeat(jnp.exp(steps), dims[position] // blocks).reshape((-1,) + (1,) * (len(dims) - 1 - position))
    return level


def noise(stream_key, shape, deviation, bound, shards=(), held_as=jnp.bfloat16):
    level = level_of(stream_key, shape, shards, -0.22, 0.18) if shards else 1.0
    result = jax.random.normal(stream_key, shape, jnp.float32) * deviation * level
    return jnp.minimum(jnp.maximum(result, -bound), bound).astype(held_as)


def setup_inputs(seed: int = 0) -> dict:
    arg_keys = jax.random.split(jax.random.key(seed), 7)
    tokens = noise(arg_keys[0], (TOKENS, D), 1.0, 6.0, ((0, 8), (1, 16)), jnp.float32)
    layer_norm_gain = jnp.clip(1.0 + 0.18 * jax.random.normal(arg_keys[1], (D,), jnp.float32), 0.1, 1.9)
    gate_alpha = jnp.clip(jax.random.uniform(arg_keys[2], (1,), jnp.float32, 0.3, 1.2), 0.3, 1.2)
    weight_in = noise(arg_keys[3], (D, FF), D ** -0.5, 0.0625, ((0, 16), (1, 8)), jnp.float32)
    weight_out = noise(arg_keys[4], (FF, D), FF ** -0.5, 0.046875, ((0, 8), (1, 16)), jnp.float32)
    output_gradient = noise(arg_keys[5], (TOKENS, D), 1.0, 6.0, ((0, 8), (1, 16)), jnp.float32)
    return dict(tokens=tokens, layer_norm_gain=layer_norm_gain, gate_alpha=gate_alpha, weight_in=weight_in, weight_out=weight_out, output_gradient=output_gradient)


epsilon = 1e-05
gelu_scale = 0.7978845608028654
cubic = 0.044715

def matmul(left, right, left_dim, right_dim):
    return lax.dot_general(left, right, (((left_dim,), (right_dim,)), ((), ())), precision=lax.Precision.HIGHEST, preferred_element_type=jnp.float32)

def gelu_parts(hidden):
    inner = gelu_scale * (hidden + cubic * hidden * hidden * hidden)
    tangent = jnp.tanh(inner)
    active = 0.5 * hidden * (1.0 + tangent)
    slope = 0.5 * (1.0 + tangent) + 0.5 * hidden * (1.0 - tangent * tangent) * gelu_scale * (1.0 + 3.0 * cubic * hidden * hidden)
    return (active, slope)

def reference(tokens, layer_norm_gain, gate_alpha, weight_in, weight_out, output_gradient):
    row_mean = lax.optimization_barrier(jnp.mean(tokens, axis=1, keepdims=True))
    centered_rows = tokens - row_mean
    variance = lax.optimization_barrier(jnp.mean(centered_rows * centered_rows, axis=1, keepdims=True))
    inverse_deviation = lax.rsqrt(variance + epsilon)
    standardized_input = centered_rows * inverse_deviation
    normalized_rows = standardized_input * layer_norm_gain[None, :]
    hidden = matmul(normalized_rows, weight_in, 1, 0)
    active, slope = gelu_parts(hidden)
    mixed = matmul(active, weight_out, 1, 0)
    gate = jnp.tanh(gate_alpha[0])
    block_out = tokens + gate * mixed
    scaled_grad = gate * output_gradient
    weight_out_grad = matmul(active, scaled_grad, 0, 0)
    hidden_grad = matmul(scaled_grad, weight_out, 1, 1) * slope
    weight_in_grad = matmul(normalized_rows, hidden_grad, 0, 0)
    normalized_gradient = matmul(hidden_grad, weight_in, 1, 1)
    norm_gain_gradient = lax.optimization_barrier(jnp.sum(normalized_gradient * standardized_input, axis=0))
    scaled_rows = normalized_gradient * layer_norm_gain[None, :]
    plain_mean_value = lax.optimization_barrier(jnp.mean(scaled_rows, axis=1, keepdims=True))
    cross_mean_value = lax.optimization_barrier(jnp.mean(scaled_rows * standardized_input, axis=1, keepdims=True))
    token_gradient = output_gradient + inverse_deviation * (scaled_rows - plain_mean_value - standardized_input * cross_mean_value)
    return (block_out, token_gradient, weight_in_grad, weight_out_grad, norm_gain_gradient)
```

```python
import jax
import jax.numpy as jnp
from jax import lax
from jax.sharding import PartitionSpec as P

D = 8192
SIDE = 4

epsilon = 1e-05
gelu_scale = 0.7978845608028654
cubic = 0.044715


def matmul(left, right, left_dim, right_dim):
    return lax.dot_general(
        left,
        right,
        (((left_dim,), (right_dim,)), ((), ())),
        precision=lax.Precision.HIGH,
        preferred_element_type=jnp.float32,
    )


def gelu_parts(hidden):
    inner = gelu_scale * (hidden + cubic * hidden * hidden * hidden)
    tangent = jnp.tanh(inner)
    active = 0.5 * hidden * (1.0 + tangent)
    slope = 0.5 * (1.0 + tangent) + 0.5 * hidden * (1.0 - tangent * tangent) * gelu_scale * (
        1.0 + 3.0 * cubic * hidden * hidden
    )
    return (active, slope)


def shift_x(value, step):
    pairs = [(x * 4 + y, (x + step) % 4 * 4 + y) for x in range(4) for y in range(4)]
    return lax.ppermute(value, "col", pairs)


def shift_y(value, step):
    pairs = [(x * 4 + y, x * 4 + (y + step) % 4) for x in range(4) for y in range(4)]
    return lax.ppermute(value, "col", pairs)


def shift_z(value, step):
    pairs = [(z * 2 + core, (z + step) % 4 * 2 + core) for z in range(4) for core in range(2)]
    return lax.ppermute(value, "row", pairs)


def swap_core(value):
    return lax.ppermute(value, "row", [(i, i ^ 1) for i in range(8)])


def halves(value, axis):
    middle = value.shape[axis] // 2
    return (
        lax.slice_in_dim(value, 0, middle, axis=axis),
        lax.slice_in_dim(value, middle, value.shape[axis], axis=axis),
    )


def scatter_ring(blocks, shift, axis):
    low, high = halves(blocks[2], axis)
    from_behind, from_ahead = shift(low, 1), shift(high, -1)
    one, three = halves(blocks[1], axis), halves(blocks[3], axis)
    ahead = jnp.concatenate([one[0] + from_behind, one[1]], axis=axis)
    behind = jnp.concatenate([three[0], three[1] + from_ahead], axis=axis)
    return blocks[0] + shift(ahead, 1) + shift(behind, -1)


def gather_ring(value, shift, axis):
    behind, ahead = shift(value, 1), shift(value, -1)
    far_low = shift(halves(behind, axis)[0], 1)
    far_high = shift(halves(ahead, axis)[1], -1)
    return [value, ahead, jnp.concatenate([far_low, far_high], axis=axis), behind]


def scatter_direct(blocks, shift):
    return blocks[0] + shift(blocks[1], 1) + shift(blocks[3], -1) + shift(blocks[2], 2)


def ring_of(value, shift):
    return jnp.stack([value, shift(value, -1), shift(value, 2), shift(value, 1)])


def scatter_plane(value, first, second, x_first):
    grid = value.reshape((4, 4) + (value.shape[0] // 16, value.shape[1]))
    blocks = [grid[i] if x_first else grid[:, i] for i in range(4)]
    mine = scatter_ring(blocks, first, 2)
    return scatter_direct([mine[i] for i in range(4)], second)


def gather_plane(value, first, second, x_first):
    one = ring_of(value, first)
    two = jnp.stack(gather_ring(one, second, 2))
    if x_first:
        two = jnp.swapaxes(two, 0, 1)
    return two.reshape((-1, value.shape[1]))


def tie(value, *after):
    return lax.optimization_barrier((value, after))[0]


def merge(stats, rows, count):
    means, spreads = stats[:, :rows], stats[:, rows : 2 * rows]
    mean = jnp.mean(means, axis=0)
    spread = jnp.sum(spreads, axis=0) + count * jnp.sum(jnp.square(means - mean), axis=0)
    return jnp.concatenate([mean, spread, jnp.sum(stats[:, 2 * rows :], axis=0)])


def sum_row(value):
    value = value + swap_core(value)
    value = value + shift_z(value, 2)
    return value + shift_z(value, 1)


def near_row(value):
    return [value, shift_z(value, -1), shift_z(value, 1)]


def far_row(near):
    low, high = halves(near[2], 0)[0], halves(near[1], 0)[1]
    return jnp.concatenate([shift_z(low, 1), shift_z(high, -1)], axis=0)


def whole_row(near, far, core, start):
    near = jnp.stack(near)
    near_other, far_other = swap_core(near), swap_core(far)
    ring = jnp.stack([near[0], near[1], far, near[2]])
    other = jnp.stack([near_other[0], near_other[1], far_other, near_other[2]])
    both = jnp.where(core == 0, jnp.stack([ring, other], axis=1), jnp.stack([other, ring], axis=1))
    both = lax.dynamic_slice_in_dim(jnp.concatenate([both, both[:3]], axis=0), start, 4, axis=0)
    return both.reshape((-1, far.shape[1]))


def turn(value, x, y):
    grid = value.reshape((4, 4, value.shape[0] // 16, value.shape[1]))
    grid = lax.dynamic_slice_in_dim(jnp.concatenate([grid, grid[:3]], axis=0), x, 4, axis=0)
    grid = lax.dynamic_slice_in_dim(jnp.concatenate([grid, grid[:, :3]], axis=1), y, 4, axis=1)
    return grid.reshape(value.shape)


def scatter_row(value, core, start):
    grid = value.reshape((4, 2, value.shape[0] // 8, value.shape[1]))
    keep = lax.dynamic_index_in_dim(grid, core, axis=1, keepdims=False)
    give = lax.dynamic_index_in_dim(grid, 1 - core, axis=1, keepdims=False)
    keep = keep + swap_core(give)
    keep = lax.dynamic_slice_in_dim(jnp.concatenate([keep, keep[:3]], axis=0), start, 4, axis=0)
    return scatter_ring([keep[i] for i in range(4)], shift_z, 0)


def shards(tokens, layer_norm_gain, gate_alpha, weight_in, weight_out, output_gradient):
    row, col = lax.axis_index("row"), lax.axis_index("col")
    z, core = row // 2, row % 2
    x, y = col // 4, col % 4
    gain = layer_norm_gain[None, :]
    panel = tokens.shape[1]
    half = weight_in.shape[1] // 2
    gate = jnp.tanh(gate_alpha[0])

    order = ((shift_x, shift_y, True), (shift_y, shift_x, False))

    near = near_row(gate * output_gradient)
    rows = tokens.shape[0]
    local_mean = jnp.mean(tokens, axis=1)
    local_spread = jnp.sum(jnp.square(tokens - local_mean[:, None]), axis=1)
    gain_out = jnp.sum(weight_in * layer_norm_gain[:, None], axis=0)
    stats = ring_of(jnp.concatenate([local_mean, local_spread, gain_out]), shift_x)
    near, stats = lax.optimization_barrier((near, stats))
    far = far_row(near)
    stats = ring_of(merge(stats, rows, panel), shift_y)
    far, stats = lax.optimization_barrier((far, stats))
    stats = merge(stats, rows, 4 * panel)
    gain_out = stats[2 * rows :]
    stats = stats[: 2 * rows].reshape(2, rows)
    inverse_deviation = lax.rsqrt(stats[1] / D + epsilon)[:, None]
    standardized = (tokens - stats[0][:, None]) * inverse_deviation
    normed = standardized * gain
    normed_near = near_row(normed)
    grad_all = tie(whole_row(near, far, core, (4 - z) % 4), normed_near)

    active_grad_part = matmul(grad_all, weight_out, 1, 1)
    active_grad = lax.psum_scatter(active_grad_part, "col", scatter_dimension=0, tiled=True)

    normed_near, _ = lax.optimization_barrier((normed_near, active_grad_part))
    normed_all = whole_row(normed_near, far_row(normed_near), core, (4 - z) % 4)
    normed_turned = turn(normed_all, x, y)
    hidden = jnp.concatenate(
        [
            scatter_plane(matmul(normed_turned, weight_in[:, i * half : (i + 1) * half], 1, 0), *order[i])
            for i in range(2)
        ],
        axis=1,
    )
    active, slope = gelu_parts(hidden)
    ones = [ring_of(active[:, i * half : (i + 1) * half], order[i][0]) for i in range(2)]
    hidden_grad = active_grad * slope
    hidden_grad_all = lax.all_gather(hidden_grad, "col", axis=0, tiled=True)
    grad_turned = turn(tie(grad_all, ones), x, y)
    twos = [jnp.stack(gather_ring(ones[i], order[i][1], 2)) for i in range(2)]
    active_all = jnp.concatenate(
        [jnp.swapaxes(twos[0], 0, 1).reshape(-1, half), twos[1].reshape(-1, half)], axis=1
    )

    totals = jnp.stack([jnp.sum(hidden_grad * gain_out, axis=1), jnp.sum(hidden_grad * hidden, axis=1)])
    totals = ring_of(sum_row(totals), shift_x)
    totals = lax.dynamic_index_in_dim(totals, (4 + z - x) % 4, axis=0, keepdims=False)
    totals = ring_of(totals, shift_y)
    totals = jnp.concatenate(
        [
            lax.dynamic_index_in_dim(totals, (4 + 2 * core + i - y) % 4, axis=0, keepdims=False)
            for i in range(2)
        ],
        axis=1,
    )

    mixed_part = matmul(active_all, weight_out, 1, 0)
    active_all = tie(active_all, mixed_part)
    mixed = lax.psum_scatter(
        turn(mixed_part, (4 - x) % 4, (4 - y) % 4), "row", scatter_dimension=0, tiled=True
    )
    block_out = tokens + gate * mixed

    hidden_grad_all = tie(hidden_grad_all, mixed_part)
    normed_grad_part = matmul(hidden_grad_all, weight_in, 1, 1)
    normed_grad_part, normed_all, hidden_grad_all = lax.optimization_barrier(
        (normed_grad_part, normed_all, hidden_grad_all)
    )
    normalized_gradient = scatter_row(normed_grad_part, core, z)
    norm_gain_gradient = sum_row(jnp.sum(normed_grad_part * normed_all, axis=0) / layer_norm_gain)
    weight_out_grad = matmul(tie(active_all, normed_grad_part), grad_turned, 0, 0)
    weight_in_grad = matmul(normed_all, hidden_grad_all, 0, 0)

    plain_mean_value = (totals[0] / D)[:, None]
    cross_mean_value = (totals[1] / D)[:, None]
    token_gradient = output_gradient + inverse_deviation * (
        normalized_gradient * gain - plain_mean_value - standardized * cross_mean_value
    )
    return (block_out, token_gradient, weight_in_grad, weight_out_grad, norm_gain_gradient)


def solution(mesh):
    return jax.shard_map(
        shards,
        mesh=mesh,
        in_specs=(
            P("row", "col"),
            P("col"),
            P(),
            P("col", "row"),
            P("row", "col"),
            P("row", "col"),
        ),
        out_specs=(P("row", "col"), P("row", "col"), P("col", "row"), P("row", "col"), P("col")),
        check_vma=False,
    )
```

```python
import jax
import jax.numpy as jnp
from jax import lax
from jax.sharding import PartitionSpec as P

D = 8192
SIDE = 4

epsilon = 1e-05
gelu_scale = 0.7978845608028654
cubic = 0.044715


def matmul(left, right, left_dim, right_dim):
    return lax.dot_general(
        left,
        right,
        (((left_dim,), (right_dim,)), ((), ())),
        precision=lax.Precision.HIGH,
        preferred_element_type=jnp.float32,
    )


def gelu_parts(hidden):
    inner = gelu_scale * (hidden + cubic * hidden * hidden * hidden)
    tangent = jnp.tanh(inner)
    active = 0.5 * hidden * (1.0 + tangent)
    slope = 0.5 * (1.0 + tangent) + 0.5 * hidden * (1.0 - tangent * tangent) * gelu_scale * (
        1.0 + 3.0 * cubic * hidden * hidden
    )
    return (active, slope)


def shift_x(value, step):
    pairs = [(x * 4 + y, (x + step) % 4 * 4 + y) for x in range(4) for y in range(4)]
    return lax.ppermute(value, "col", pairs)


def shift_y(value, step):
    pairs = [(x * 4 + y, x * 4 + (y + step) % 4) for x in range(4) for y in range(4)]
    return lax.ppermute(value, "col", pairs)


def shift_z(value, step):
    pairs = [(z * 2 + core, (z + step) % 4 * 2 + core) for z in range(4) for core in range(2)]
    return lax.ppermute(value, "row", pairs)


def swap_core(value):
    return lax.ppermute(value, "row", [(i, i ^ 1) for i in range(8)])


def halves(value, axis):
    middle = value.shape[axis] // 2
    return (
        lax.slice_in_dim(value, 0, middle, axis=axis),
        lax.slice_in_dim(value, middle, value.shape[axis], axis=axis),
    )


def scatter_ring(blocks, shift, axis):
    low, high = halves(blocks[2], axis)
    from_behind, from_ahead = shift(low, 1), shift(high, -1)
    one, three = halves(blocks[1], axis), halves(blocks[3], axis)
    ahead = jnp.concatenate([one[0] + from_behind, one[1]], axis=axis)
    behind = jnp.concatenate([three[0], three[1] + from_ahead], axis=axis)
    return blocks[0] + shift(ahead, 1) + shift(behind, -1)


def gather_first(value, shift):
    return shift(value, 1), shift(value, -1)


def gather_second(received, shift, axis):
    return shift(halves(received[0], axis)[0], 1), shift(halves(received[1], axis)[1], -1)


def scatter_direct(blocks, shift):
    return blocks[0] + shift(blocks[1], 1) + shift(blocks[3], -1) + shift(blocks[2], 2)


def ring_of(value, shift):
    return jnp.stack([value, shift(value, -1), shift(value, 2), shift(value, 1)])


def scatter_plane(value, first, second, x_first):
    grid = value.reshape((4, 4) + (value.shape[0] // 16, value.shape[1]))
    blocks = [grid[i] if x_first else grid[:, i] for i in range(4)]
    mine = scatter_ring(blocks, first, 2)
    return scatter_direct([mine[i] for i in range(4)], second)


def tie(value, *after):
    return lax.optimization_barrier((value, after))[0]


def merge(stats, rows, count):
    means, spreads = stats[:, :rows], stats[:, rows : 2 * rows]
    mean = jnp.mean(means, axis=0)
    spread = jnp.sum(spreads, axis=0) + count * jnp.sum(jnp.square(means - mean), axis=0)
    return jnp.concatenate([mean, spread, jnp.sum(stats[:, 2 * rows :], axis=0)])


def sum_row(value):
    value = value + swap_core(value)
    value = value + shift_z(value, 2)
    return value + shift_z(value, 1)


def near_row(value):
    return [value, shift_z(value, -1), shift_z(value, 1)]


def far_row(near):
    low, high = halves(near[2], 0)[0], halves(near[1], 0)[1]
    return jnp.concatenate([shift_z(low, 1), shift_z(high, -1)], axis=0)


def whole_row(near, far, core, start):
    near = jnp.stack(near)
    near_other, far_other = swap_core(near), swap_core(far)
    ring = jnp.stack([near[0], near[1], far, near[2]])
    other = jnp.stack([near_other[0], near_other[1], far_other, near_other[2]])
    both = jnp.where(core == 0, jnp.stack([ring, other], axis=1), jnp.stack([other, ring], axis=1))
    both = lax.dynamic_slice_in_dim(jnp.concatenate([both, both[:3]], axis=0), start, 4, axis=0)
    return both.reshape((-1, far.shape[1]))


def turn(value, x, y):
    grid = value.reshape((4, 4, value.shape[0] // 16, value.shape[1]))
    grid = lax.dynamic_slice_in_dim(jnp.concatenate([grid, grid[:3]], axis=0), x, 4, axis=0)
    grid = lax.dynamic_slice_in_dim(jnp.concatenate([grid, grid[:, :3]], axis=1), y, 4, axis=1)
    return grid.reshape(value.shape)


def scatter_row(value, core, start):
    grid = value.reshape((4, 2, value.shape[0] // 8, value.shape[1]))
    keep = lax.dynamic_index_in_dim(grid, core, axis=1, keepdims=False)
    give = lax.dynamic_index_in_dim(grid, 1 - core, axis=1, keepdims=False)
    keep = keep + swap_core(give)
    keep = lax.dynamic_slice_in_dim(jnp.concatenate([keep, keep[:3]], axis=0), start, 4, axis=0)
    return scatter_ring([keep[i] for i in range(4)], shift_z, 0)


def shards(tokens, layer_norm_gain, gate_alpha, weight_in, weight_out, output_gradient):
    row, col = lax.axis_index("row"), lax.axis_index("col")
    z, core = row // 2, row % 2
    x, y = col // 4, col % 4
    gain = layer_norm_gain[None, :]
    panel = tokens.shape[1]
    half = weight_in.shape[1] // 2
    gate = jnp.tanh(gate_alpha[0])

    order = ((shift_x, shift_y, True), (shift_y, shift_x, False))

    near = near_row(gate * output_gradient)
    rows = tokens.shape[0]
    local_mean = jnp.mean(tokens, axis=1)
    local_spread = jnp.sum(jnp.square(tokens - local_mean[:, None]), axis=1)
    gain_out = jnp.sum(weight_in * layer_norm_gain[:, None], axis=0)
    stats = ring_of(jnp.concatenate([local_mean, local_spread, gain_out]), shift_x)
    near, stats = lax.optimization_barrier((near, stats))
    far = far_row(near)
    stats = ring_of(merge(stats, rows, panel), shift_y)
    far, stats = lax.optimization_barrier((far, stats))
    stats = merge(stats, rows, 4 * panel)
    gain_out = stats[2 * rows :]
    stats = stats[: 2 * rows].reshape(2, rows)
    inverse_deviation = lax.rsqrt(stats[1] / D + epsilon)[:, None]
    standardized = (tokens - stats[0][:, None]) * inverse_deviation
    normed = standardized * gain
    normed_near = near_row(normed)
    grad_all = tie(whole_row(near, far, core, (4 - z) % 4), normed_near)

    active_grad_part = matmul(grad_all, weight_out, 1, 1)
    active_grad = lax.psum_scatter(active_grad_part, "col", scatter_dimension=0, tiled=True)

    normed_near, _ = lax.optimization_barrier((normed_near, active_grad_part))
    normed_all = whole_row(normed_near, far_row(normed_near), core, (4 - z) % 4)
    normed_turned = turn(normed_all, x, y)
    hidden = jnp.concatenate(
        [
            scatter_plane(matmul(normed_turned, weight_in[:, i * half : (i + 1) * half], 1, 0), *order[i])
            for i in range(2)
        ],
        axis=1,
    )
    active, slope = gelu_parts(hidden)
    ones = [ring_of(active[:, i * half : (i + 1) * half], order[i][0]) for i in range(2)]
    hidden_grad = active_grad * slope
    hidden_grad_all = lax.all_gather(hidden_grad, "col", axis=0, tiled=True)
    near = [gather_first(ones[i], order[i][1]) for i in range(2)]
    far = [gather_second(near[i], order[i][1], 2) for i in range(2)]
    grad_turned = turn(tie(grad_all, ones), x, y).reshape(4, 4, -1, panel)
    grad_turned = [jnp.swapaxes(grad_turned, 0, 1), grad_turned]
    grad_near = [jnp.stack([g[0], g[1], g[3]]).reshape(-1, panel) for g in grad_turned]
    grad_far = [g[2].reshape(-1, panel) for g in grad_turned]
    near, grad_near, grad_far = lax.optimization_barrier((near, grad_near, grad_far))
    outs, mixed_near = [], []
    for i in range(2):
        three = jnp.stack([ones[i], near[i][1], near[i][0]]).reshape(-1, half)
        mixed_near.append(matmul(three, weight_out[i * half : (i + 1) * half], 1, 0))
        outs.append(matmul(three, grad_near[i], 0, 0))
    far, outs, mixed_near = lax.optimization_barrier((far, outs, mixed_near))
    far = [jnp.concatenate(far[i], axis=2).reshape(-1, half) for i in range(2)]

    totals = jnp.stack([jnp.sum(hidden_grad * gain_out, axis=1), jnp.sum(hidden_grad * hidden, axis=1)])
    totals = ring_of(tie(sum_row(tie(totals, near)), far), shift_x)
    totals = lax.dynamic_index_in_dim(totals, (4 + z - x) % 4, axis=0, keepdims=False)
    totals = ring_of(totals, shift_y)
    totals = jnp.concatenate(
        [
            lax.dynamic_index_in_dim(totals, (4 + 2 * core + i - y) % 4, axis=0, keepdims=False)
            for i in range(2)
        ],
        axis=1,
    )

    mixed_part = []
    for i in range(2):
        part = matmul(far[i], weight_out[i * half : (i + 1) * half], 1, 0).reshape(4, -1, panel)
        kept = mixed_near[i].reshape(3, 4, -1, panel)
        mixed_part.append(jnp.stack([kept[0], kept[1], part, kept[2]]))
    mixed_part = (jnp.swapaxes(mixed_part[0], 0, 1) + mixed_part[1]).reshape(-1, panel)
    mixed = lax.psum_scatter(
        turn(mixed_part, (4 - x) % 4, (4 - y) % 4), "row", scatter_dimension=0, tiled=True
    )
    block_out = tokens + gate * mixed

    hidden_grad_all = tie(hidden_grad_all, mixed_part)
    normed_grad_part = matmul(hidden_grad_all, weight_in, 1, 1)
    normed_grad_part, normed_all, hidden_grad_all = lax.optimization_barrier(
        (normed_grad_part, normed_all, hidden_grad_all)
    )
    normalized_gradient = scatter_row(normed_grad_part, core, z)
    norm_gain_gradient = sum_row(jnp.sum(normed_grad_part * normed_all, axis=0) / layer_norm_gain)
    far = tie(far, normed_grad_part)
    weight_out_grad = jnp.concatenate([outs[i] + matmul(far[i], grad_far[i], 0, 0) for i in range(2)])
    weight_in_grad = matmul(normed_all, hidden_grad_all, 0, 0)

    plain_mean_value = (totals[0] / D)[:, None]
    cross_mean_value = (totals[1] / D)[:, None]
    token_gradient = output_gradient + inverse_deviation * (
        normalized_gradient * gain - plain_mean_value - standardized * cross_mean_value
    )
    return (block_out, token_gradient, weight_in_grad, weight_out_grad, norm_gain_gradient)


def solution(mesh):
    return jax.shard_map(
        shards,
        mesh=mesh,
        in_specs=(
            P("row", "col"),
            P("col"),
            P(),
            P("col", "row"),
            P("row", "col"),
            P("row", "col"),
        ),
        out_specs=(P("row", "col"), P("row", "col"), P("col", "row"), P("row", "col"), P("col")),
        check_vma=False,
    )
```

```python
import jax
import jax.numpy as jnp
from jax import lax
from jax.sharding import PartitionSpec as P

D = 8192
SIDE = 4

epsilon = 1e-05
gelu_scale = 0.7978845608028654
cubic = 0.044715


def matmul(left, right, left_dim, right_dim):
    return lax.dot_general(
        left,
        right,
        (((left_dim,), (right_dim,)), ((), ())),
        precision=lax.Precision.HIGH,
        preferred_element_type=jnp.float32,
    )


def gelu_parts(hidden):
    inner = gelu_scale * (hidden + cubic * hidden * hidden * hidden)
    tangent = jnp.tanh(inner)
    active = 0.5 * hidden * (1.0 + tangent)
    slope = 0.5 * (1.0 + tangent) + 0.5 * hidden * (1.0 - tangent * tangent) * gelu_scale * (
        1.0 + 3.0 * cubic * hidden * hidden
    )
    return (active, slope)


def shift_x(value, step):
    pairs = [(x * 4 + y, (x + step) % 4 * 4 + y) for x in range(4) for y in range(4)]
    return lax.ppermute(value, "col", pairs)


def shift_y(value, step):
    pairs = [(x * 4 + y, x * 4 + (y + step) % 4) for x in range(4) for y in range(4)]
    return lax.ppermute(value, "col", pairs)


def shift_z(value, step):
    pairs = [(z * 2 + core, (z + step) % 4 * 2 + core) for z in range(4) for core in range(2)]
    return lax.ppermute(value, "row", pairs)


def swap_core(value):
    return lax.ppermute(value, "row", [(i, i ^ 1) for i in range(8)])


def halves(value, axis):
    middle = value.shape[axis] // 2
    return (
        lax.slice_in_dim(value, 0, middle, axis=axis),
        lax.slice_in_dim(value, middle, value.shape[axis], axis=axis),
    )


def scatter_ring(blocks, shift, axis):
    low, high = halves(blocks[2], axis)
    from_behind, from_ahead = shift(low, 1), shift(high, -1)
    one, three = halves(blocks[1], axis), halves(blocks[3], axis)
    ahead = jnp.concatenate([one[0] + from_behind, one[1]], axis=axis)
    behind = jnp.concatenate([three[0], three[1] + from_ahead], axis=axis)
    return blocks[0] + shift(ahead, 1) + shift(behind, -1)


def gather_first(value, shift):
    return shift(value, 1), shift(value, -1)


def gather_second(received, shift, axis):
    return shift(halves(received[0], axis)[0], 1), shift(halves(received[1], axis)[1], -1)


def scatter_direct(blocks, shift):
    return blocks[0] + shift(blocks[1], 1) + shift(blocks[3], -1) + shift(blocks[2], 2)


def ring_of(value, shift):
    return jnp.stack([value, shift(value, -1), shift(value, 2), shift(value, 1)])


def scatter_plane(value, first, second, x_first):
    grid = value.reshape((4, 4) + (value.shape[0] // 16, value.shape[1]))
    blocks = [grid[i] if x_first else grid[:, i] for i in range(4)]
    mine = scatter_ring(blocks, first, 2)
    return scatter_direct([mine[i] for i in range(4)], second)


def tie(value, *after):
    return lax.optimization_barrier((value, after))[0]


def merge(stats, rows, count):
    means, spreads = stats[:, :rows], stats[:, rows : 2 * rows]
    mean = jnp.mean(means, axis=0)
    spread = jnp.sum(spreads, axis=0) + count * jnp.sum(jnp.square(means - mean), axis=0)
    return jnp.concatenate([mean, spread, jnp.sum(stats[:, 2 * rows :], axis=0)])


def sum_row(value):
    value = value + swap_core(value)
    value = value + shift_z(value, 2)
    return value + shift_z(value, 1)


def near_row(value):
    return [value, shift_z(value, -1), shift_z(value, 1)]


def far_row(near):
    low, high = halves(near[2], 0)[0], halves(near[1], 0)[1]
    return jnp.concatenate([shift_z(low, 1), shift_z(high, -1)], axis=0)


def whole_row(near, far, core, start):
    near = jnp.stack(near)
    near_other, far_other = swap_core(near), swap_core(far)
    ring = jnp.stack([near[0], near[1], far, near[2]])
    other = jnp.stack([near_other[0], near_other[1], far_other, near_other[2]])
    both = jnp.where(core == 0, jnp.stack([ring, other], axis=1), jnp.stack([other, ring], axis=1))
    both = lax.dynamic_slice_in_dim(jnp.concatenate([both, both[:3]], axis=0), start, 4, axis=0)
    return both.reshape((-1, far.shape[1]))


def turn(value, x, y):
    grid = value.reshape((4, 4, value.shape[0] // 16, value.shape[1]))
    grid = lax.dynamic_slice_in_dim(jnp.concatenate([grid, grid[:3]], axis=0), x, 4, axis=0)
    grid = lax.dynamic_slice_in_dim(jnp.concatenate([grid, grid[:, :3]], axis=1), y, 4, axis=1)
    return grid.reshape(value.shape)


def swap_halves(value, core, start):
    grid = value.reshape((4, 2, value.shape[0] // 8, value.shape[1]))
    keep = lax.dynamic_index_in_dim(grid, core, axis=1, keepdims=False)
    give = lax.dynamic_index_in_dim(grid, 1 - core, axis=1, keepdims=False)
    keep = keep + swap_core(give)
    return lax.dynamic_slice_in_dim(jnp.concatenate([keep, keep[:3]], axis=0), start, 4, axis=0)


def shards(tokens, layer_norm_gain, gate_alpha, weight_in, weight_out, output_gradient):
    row, col = lax.axis_index("row"), lax.axis_index("col")
    z, core = row // 2, row % 2
    x, y = col // 4, col % 4
    gain = layer_norm_gain[None, :]
    panel = tokens.shape[1]
    half = weight_in.shape[1] // 2
    gate = jnp.tanh(gate_alpha[0])

    order = ((shift_x, shift_y, True), (shift_y, shift_x, False))

    scaled_grad = gate * output_gradient
    near = near_row(scaled_grad)
    rows = tokens.shape[0]
    local_mean = jnp.mean(tokens, axis=1)
    local_spread = jnp.sum(jnp.square(tokens - local_mean[:, None]), axis=1)
    gain_out = jnp.sum(weight_in * layer_norm_gain[:, None], axis=0)
    stats = tie(jnp.concatenate([local_mean, local_spread, gain_out]), near)
    far = far_row(near)
    stats = merge(ring_of(stats, shift_x), rows, panel)
    near = tie(near, stats)
    stats = merge(ring_of(stats, shift_y), rows, 4 * panel)
    gain_out = stats[2 * rows :]
    stats = stats[: 2 * rows].reshape(2, rows)
    inverse_deviation = lax.rsqrt(stats[1] / D + epsilon)[:, None]
    standardized = (tokens - stats[0][:, None]) * inverse_deviation
    normed = standardized * gain
    normed_near = near_row(normed)
    grad_all = whole_row(near, far, core, (4 - z) % 4)

    active_grad_part = matmul(grad_all, weight_out, 1, 1)
    active_grad = lax.psum_scatter(active_grad_part, "col", scatter_dimension=0, tiled=True)

    normed_near, _ = lax.optimization_barrier((normed_near, active_grad_part))
    normed_all = whole_row(normed_near, far_row(normed_near), core, (4 - z) % 4)
    normed_turned = turn(normed_all, x, y)
    hidden = jnp.concatenate(
        [
            scatter_plane(matmul(normed_turned, weight_in[:, i * half : (i + 1) * half], 1, 0), *order[i])
            for i in range(2)
        ],
        axis=1,
    )
    active, slope = gelu_parts(hidden)
    ones = [ring_of(active[:, i * half : (i + 1) * half], order[i][0]) for i in range(2)]
    hidden_grad = active_grad * slope
    hidden_grad_all = lax.all_gather(hidden_grad, "col", axis=0, tiled=True)
    near = [gather_first(ones[i], order[i][1]) for i in range(2)]
    far = [gather_second(near[i], order[i][1], 2) for i in range(2)]
    grad_turned = turn(tie(grad_all, ones), x, y).reshape(4, 4, -1, panel)
    grad_turned = [jnp.swapaxes(grad_turned, 0, 1), grad_turned]
    grad_near = [jnp.stack([g[0], g[1], g[3]]).reshape(-1, panel) for g in grad_turned]
    grad_far = [g[2].reshape(-1, panel) for g in grad_turned]
    near, grad_near, grad_far = lax.optimization_barrier((near, grad_near, grad_far))
    outs, mixed_near = [], []
    for i in range(2):
        three = jnp.stack([ones[i], near[i][1], near[i][0]]).reshape(-1, half)
        mixed_near.append(matmul(three, weight_out[i * half : (i + 1) * half], 1, 0))
        outs.append(matmul(three, grad_near[i], 0, 0))
    far, outs, mixed_near = lax.optimization_barrier((far, outs, mixed_near))
    far = [jnp.concatenate(far[i], axis=2).reshape(-1, half) for i in range(2)]

    totals = jnp.stack([jnp.sum(hidden_grad * gain_out, axis=1), jnp.sum(hidden_grad * hidden, axis=1)])
    totals = ring_of(tie(sum_row(tie(totals, near)), far), shift_x)
    totals = lax.dynamic_index_in_dim(totals, (4 + z - x) % 4, axis=0, keepdims=False)
    totals = ring_of(totals, shift_y)
    totals = jnp.concatenate(
        [
            lax.dynamic_index_in_dim(totals, (4 + 2 * core + i - y) % 4, axis=0, keepdims=False)
            for i in range(2)
        ],
        axis=1,
    )

    mixed_part = []
    for i in range(2):
        part = matmul(far[i], weight_out[i * half : (i + 1) * half], 1, 0).reshape(4, -1, panel)
        kept = mixed_near[i].reshape(3, 4, -1, panel)
        mixed_part.append(jnp.stack([kept[0], kept[1], part, kept[2]]))
    mixed_part = (jnp.swapaxes(mixed_part[0], 0, 1) + mixed_part[1]).reshape(-1, panel)
    mixed = lax.psum_scatter(
        turn(mixed_part, (4 - x) % 4, (4 - y) % 4), "row", scatter_dimension=0, tiled=True
    )
    block_out = tokens + gate * mixed

    hidden_grad_all = tie(hidden_grad_all, mixed_part)
    normed_grad_part = matmul(hidden_grad_all, weight_in, 1, 1)
    normed_grad_part, normed_all, hidden_grad_all = lax.optimization_barrier(
        (normed_grad_part, normed_all, hidden_grad_all)
    )
    kept = swap_halves(normed_grad_part, core, z)
    norm_gain_gradient = sum_row(jnp.sum(normed_grad_part * normed_all, axis=0) / layer_norm_gain)
    far = tie(far, normed_grad_part)
    weight_out_grad = jnp.concatenate([outs[i] + matmul(far[i], grad_far[i], 0, 0) for i in range(2)])
    kept, weight_out_grad = lax.optimization_barrier((kept, weight_out_grad))
    normalized_gradient = scatter_direct([kept[i] for i in range(4)], shift_z)
    weight_in_grad = matmul(normed_all, tie(hidden_grad_all, kept), 0, 0)
    plain_mean_value = (totals[0] / D)[:, None]
    cross_mean_value = (totals[1] / D)[:, None]
    token_gradient = output_gradient + inverse_deviation * (
        normalized_gradient * gain - plain_mean_value - standardized * cross_mean_value
    )
    return (block_out, token_gradient, weight_in_grad, weight_out_grad, norm_gain_gradient)


def solution(mesh):
    return jax.shard_map(
        shards,
        mesh=mesh,
        in_specs=(
            P("row", "col"),
            P("col"),
            P(),
            P("col", "row"),
            P("row", "col"),
            P("row", "col"),
        ),
        out_specs=(P("row", "col"), P("row", "col"), P("col", "row"), P("row", "col"), P("col")),
        check_vma=False,
    )
```

```python
import jax
import jax.numpy as jnp
from jax import lax
from jax.sharding import PartitionSpec as P

D = 8192
SIDE = 4

epsilon = 1e-05
gelu_scale = 0.7978845608028654
cubic = 0.044715


def matmul(left, right, left_dim, right_dim):
    return lax.dot_general(
        left,
        right,
        (((left_dim,), (right_dim,)), ((), ())),
        precision=lax.Precision.HIGH,
        preferred_element_type=jnp.float32,
    )


def gelu_parts(hidden):
    inner = gelu_scale * (hidden + cubic * hidden * hidden * hidden)
    tangent = jnp.tanh(inner)
    active = 0.5 * hidden * (1.0 + tangent)
    slope = 0.5 * (1.0 + tangent) + 0.5 * hidden * (1.0 - tangent * tangent) * gelu_scale * (
        1.0 + 3.0 * cubic * hidden * hidden
    )
    return (active, slope)


def shift_x(value, step):
    pairs = [(x * 4 + y, (x + step) % 4 * 4 + y) for x in range(4) for y in range(4)]
    return lax.ppermute(value, "col", pairs)


def shift_y(value, step):
    pairs = [(x * 4 + y, x * 4 + (y + step) % 4) for x in range(4) for y in range(4)]
    return lax.ppermute(value, "col", pairs)


def shift_z(value, step):
    pairs = [(z * 2 + core, (z + step) % 4 * 2 + core) for z in range(4) for core in range(2)]
    return lax.ppermute(value, "row", pairs)


def swap_core(value):
    return lax.ppermute(value, "row", [(i, i ^ 1) for i in range(8)])


def halves(value, axis):
    middle = value.shape[axis] // 2
    return (
        lax.slice_in_dim(value, 0, middle, axis=axis),
        lax.slice_in_dim(value, middle, value.shape[axis], axis=axis),
    )


def scatter_ring(blocks, shift, axis):
    low, high = halves(blocks[2], axis)
    from_behind, from_ahead = shift(low, 1), shift(high, -1)
    one, three = halves(blocks[1], axis), halves(blocks[3], axis)
    ahead = jnp.concatenate([one[0] + from_behind, one[1]], axis=axis)
    behind = jnp.concatenate([three[0], three[1] + from_ahead], axis=axis)
    return blocks[0] + shift(ahead, 1) + shift(behind, -1)


def gather_first(value, shift):
    return shift(value, 1), shift(value, -1)


def gather_second(received, shift, axis):
    return shift(halves(received[0], axis)[0], 1), shift(halves(received[1], axis)[1], -1)


def scatter_direct(blocks, shift):
    return blocks[0] + shift(blocks[1], 1) + shift(blocks[3], -1) + shift(blocks[2], 2)


def ring_of(value, shift):
    return jnp.stack([value, shift(value, -1), shift(value, 2), shift(value, 1)])


def scatter_plane(value, first, second, x_first):
    grid = value.reshape((4, 4) + (value.shape[0] // 16, value.shape[1]))
    blocks = [grid[i] if x_first else grid[:, i] for i in range(4)]
    mine = scatter_ring(blocks, first, 2)
    return scatter_direct([mine[i] for i in range(4)], second)


def tie(value, *after):
    return lax.optimization_barrier((value, after))[0]


def merge(stats, count):
    mean = jnp.mean(stats[:, 0], axis=0)
    spread = jnp.sum(stats[:, 1], axis=0) + count * jnp.sum(jnp.square(stats[:, 0] - mean), axis=0)
    return jnp.stack([mean, spread])


def sum_plane(value):
    return jnp.sum(ring_of(jnp.sum(ring_of(value, shift_x), axis=0), shift_y), axis=0)


def sum_row(value):
    value = value + swap_core(value)
    value = value + shift_z(value, 2)
    return value + shift_z(value, 1)


def near_row(value):
    return [value, shift_z(value, -1), shift_z(value, 1)]


def far_row(near):
    low, high = halves(near[2], 0)[0], halves(near[1], 0)[1]
    return jnp.concatenate([shift_z(low, 1), shift_z(high, -1)], axis=0)


def whole_row(near, far, core, start):
    near = jnp.stack(near)
    near_other, far_other = swap_core(near), swap_core(far)
    ring = jnp.stack([near[0], near[1], far, near[2]])
    other = jnp.stack([near_other[0], near_other[1], far_other, near_other[2]])
    both = jnp.where(core == 0, jnp.stack([ring, other], axis=1), jnp.stack([other, ring], axis=1))
    both = lax.dynamic_slice_in_dim(jnp.concatenate([both, both[:3]], axis=0), start, 4, axis=0)
    return both.reshape((-1, far.shape[1]))


def turn(value, x, y):
    grid = value.reshape((4, 4, value.shape[0] // 16, value.shape[1]))
    grid = lax.dynamic_slice_in_dim(jnp.concatenate([grid, grid[:3]], axis=0), x, 4, axis=0)
    grid = lax.dynamic_slice_in_dim(jnp.concatenate([grid, grid[:, :3]], axis=1), y, 4, axis=1)
    return grid.reshape(value.shape)


def swap_halves(value, core, start):
    grid = value.reshape((4, 2, value.shape[0] // 8, value.shape[1]))
    keep = lax.dynamic_index_in_dim(grid, core, axis=1, keepdims=False)
    give = lax.dynamic_index_in_dim(grid, 1 - core, axis=1, keepdims=False)
    keep = keep + swap_core(give)
    return lax.dynamic_slice_in_dim(jnp.concatenate([keep, keep[:3]], axis=0), start, 4, axis=0)


def shards(tokens, layer_norm_gain, gate_alpha, weight_in, weight_out, output_gradient):
    row, col = lax.axis_index("row"), lax.axis_index("col")
    z, core = row // 2, row % 2
    x, y = col // 4, col % 4
    gain = layer_norm_gain[None, :]
    panel = tokens.shape[1]
    half = weight_in.shape[1] // 2
    gate = jnp.tanh(gate_alpha[0])

    order = ((shift_x, shift_y, True), (shift_y, shift_x, False))

    scaled_grad = gate * output_gradient
    near = near_row(scaled_grad)
    local_mean = jnp.mean(tokens, axis=1)
    local_spread = jnp.sum(jnp.square(tokens - local_mean[:, None]), axis=1)
    stats = tie(jnp.stack([local_mean, local_spread]), near)
    far = far_row(near)
    stats = merge(ring_of(stats, shift_x), panel)
    near = tie(near, stats)
    stats = merge(ring_of(stats, shift_y), 4 * panel)
    inverse_deviation = lax.rsqrt(stats[1] / D + epsilon)[:, None]
    standardized = (tokens - stats[0][:, None]) * inverse_deviation
    normed = standardized * gain
    normed_near = near_row(normed)
    grad_all = whole_row(near, far, core, (4 - z) % 4)

    active_grad_part = matmul(grad_all, weight_out, 1, 1)
    active_grad = lax.psum_scatter(active_grad_part, "col", scatter_dimension=0, tiled=True)

    normed_near, _ = lax.optimization_barrier((normed_near, active_grad_part))
    normed_all = whole_row(normed_near, far_row(normed_near), core, (4 - z) % 4)
    normed_turned = turn(normed_all, x, y)
    hidden = jnp.concatenate(
        [
            scatter_plane(matmul(normed_turned, weight_in[:, i * half : (i + 1) * half], 1, 0), *order[i])
            for i in range(2)
        ],
        axis=1,
    )
    active, slope = gelu_parts(hidden)
    ones = [ring_of(active[:, i * half : (i + 1) * half], order[i][0]) for i in range(2)]
    hidden_grad = active_grad * slope
    hidden_grad_all = lax.all_gather(hidden_grad, "col", axis=0, tiled=True)
    near = [gather_first(ones[i], order[i][1]) for i in range(2)]
    far = [gather_second(near[i], order[i][1], 2) for i in range(2)]
    grad_turned = turn(tie(grad_all, ones), x, y).reshape(4, 4, -1, panel)
    grad_turned = [jnp.swapaxes(grad_turned, 0, 1), grad_turned]
    grad_near = [jnp.stack([g[0], g[1], g[3]]).reshape(-1, panel) for g in grad_turned]
    grad_far = [g[2].reshape(-1, panel) for g in grad_turned]
    near, grad_near, grad_far = lax.optimization_barrier((near, grad_near, grad_far))
    outs, mixed_near = [], []
    for i in range(2):
        three = jnp.stack([ones[i], near[i][1], near[i][0]]).reshape(-1, half)
        mixed_near.append(matmul(three, weight_out[i * half : (i + 1) * half], 1, 0))
        outs.append(matmul(three, grad_near[i], 0, 0))
    far, outs, mixed_near = lax.optimization_barrier((far, outs, mixed_near))
    far = [jnp.concatenate(far[i], axis=2).reshape(-1, half) for i in range(2)]

    mixed_part = []
    for i in range(2):
        part = matmul(far[i], weight_out[i * half : (i + 1) * half], 1, 0).reshape(4, -1, panel)
        kept = mixed_near[i].reshape(3, 4, -1, panel)
        mixed_part.append(jnp.stack([kept[0], kept[1], part, kept[2]]))
    mixed_part = (jnp.swapaxes(mixed_part[0], 0, 1) + mixed_part[1]).reshape(-1, panel)
    mixed = lax.psum_scatter(
        turn(mixed_part, (4 - x) % 4, (4 - y) % 4), "row", scatter_dimension=0, tiled=True
    )
    block_out = tokens + gate * mixed

    hidden_grad_all = tie(hidden_grad_all, mixed_part)
    normed_grad_part = matmul(hidden_grad_all, weight_in, 1, 1)
    normed_grad_part, normed_all, hidden_grad_all = lax.optimization_barrier(
        (normed_grad_part, normed_all, hidden_grad_all)
    )
    kept = swap_halves(normed_grad_part, core, z)
    norm_gain_gradient = sum_row(jnp.sum(normed_grad_part * normed_all, axis=0) / layer_norm_gain)
    far = tie(far, normed_grad_part)
    weight_out_grad = jnp.concatenate([outs[i] + matmul(far[i], grad_far[i], 0, 0) for i in range(2)])
    normalized_gradient = scatter_direct([kept[i] for i in range(4)], shift_z)
    weight_in_grad = matmul(normed_all, tie(hidden_grad_all, kept), 0, 0)
    scaled_rows = normalized_gradient * gain
    totals = sum_plane(
        jnp.stack([jnp.sum(scaled_rows, axis=1), jnp.sum(scaled_rows * standardized, axis=1)])
    )
    plain_mean_value = (totals[0] / D)[:, None]
    cross_mean_value = (totals[1] / D)[:, None]
    token_gradient = output_gradient + inverse_deviation * (
        scaled_rows - plain_mean_value - standardized * cross_mean_value
    )
    return (block_out, token_gradient, weight_in_grad, weight_out_grad, norm_gain_gradient)


def solution(mesh):
    return jax.shard_map(
        shards,
        mesh=mesh,
        in_specs=(
            P("row", "col"),
            P("col"),
            P(),
            P("col", "row"),
            P("row", "col"),
            P("row", "col"),
        ),
        out_specs=(P("row", "col"), P("row", "col"), P("col", "row"), P("row", "col"), P("col")),
        check_vma=False,
    )
```
